256 devices in a mesh: row: 16 (over y, x), col: 16 (over z, core).
Axes of the slice: x: 4, y: 4, z: 8, core: 2. Of those that a mesh axis runs over, the one named last changes fastest.
Arguments:
- a_vals: bfloat16 [256, 64, 256, 256], P('row', 'col'), may hold values from -0.1875 to 0.1875
- a_cols: int32 [256, 64], P('row', 'col'), may hold values from 0 to 15
- p_vals: bfloat16 [256, 256, 512], P(('row', 'col')), may hold values from -0.375 to 0.375
Outputs:
- coarse: float32 [8192, 8192], P('row', 'col')
The draws below stay inside these ranges and needn't reach their ends.
All inputs are finite; a program needn't handle non-finite values.
Results may differ from the reference program's by a relative error of at most 0.0029.
Values may be sent and summed in bfloat16 or wider, within the bound.
A program may use at most 192 MiB of HBM per device.

```python
import jax
import jax.numpy as jnp
from jax import lax

BLOCK = 256
ROW_BLOCKS = 16
SLOTS = 4
RGROUPS = 16
CGROUPS = 16
PB = 1
NB = 256
CR = 2
NC = 32
CB = 16


def set_ends(values, own_key, low, top_value):
    longest = values.shape.index(max(values.shape))
    spots = []
    for shift in (0, 1):
        where = [jax.random.randint(jax.random.fold_in(own_key, axis), (), 0, length) for axis, length in enumerate(values.shape)]
        where[longest] = (where[longest] + shift) % values.shape[longest]
        spots.append(tuple(where))
    return values.at[spots[0]].set(low).at[spots[1]].set(top_value)


def steps_of(own_key, shape, shards, smallest, largest):
    def one(axis_at, shards_of):
        heights = jax.random.uniform(jax.random.fold_in(jax.random.fold_in(own_key, 6), axis_at), (shards_of,), jnp.float32, smallest / len(shards), largest / len(shards))
        return jnp.repeat(jnp.exp(heights), shape[axis_at] // shards_of).reshape((-1,) + (1,) * (len(shape) - axis_at - 1))

    gain = one(*shards[0])
    for cut in shards[1:]:
        gain = gain * one(*cut)
    return gain


def bell_draw(own_key, dims, spread, most, pieces=(), kind=jnp.bfloat16):
    entries = jax.random.normal(own_key, dims, jnp.float32) * spread
    if len(pieces) > 0:
        entries = steps_of(own_key, dims, pieces, -0.22, 0.18) * entries
    return jnp.clip(entries, min=-most, max=most).astype(kind)


def setup_inputs(seed: int = 0) -> dict:
    splits = jax.random.split(jax.random.key(seed), 4)
    return {
        "a_vals": bell_draw(splits[0], (NB, CGROUPS * SLOTS, BLOCK, BLOCK), (ROW_BLOCKS * SLOTS * CGROUPS) ** -0.5, 0.1875, ((0, 16), (1, 16))),
        "a_cols": set_ends(jax.random.randint(splits[1], (NB, CGROUPS * SLOTS), 0, CB), jax.random.fold_in(splits[1], 1), 0, CB - 1).astype(jnp.int32),
        "p_vals": bell_draw(splits[2], (NB, BLOCK, CR * BLOCK), BLOCK ** -0.5, 0.375, ((0, 256),)),
    }


def reference(a_vals, a_cols, p_vals):
    coarse_width = CR * BLOCK
    slot_count = CGROUPS * SLOTS
    slot_group = jnp.arange(slot_count, dtype=jnp.int32) // SLOTS
    p_full = p_vals.astype(jnp.float32).reshape(RGROUPS, ROW_BLOCKS, BLOCK, coarse_width)

    def group_rows(group_index):
        first_row = group_index * ROW_BLOCKS
        rows_a = lax.dynamic_slice_in_dim(a_vals, first_row, ROW_BLOCKS, 0)
        rows_c = lax.dynamic_slice_in_dim(a_cols, first_row, ROW_BLOCKS, 0)
        rows_p = lax.dynamic_slice_in_dim(p_vals, first_row, ROW_BLOCKS, 0)

        def add_row(partial_sums, item):
            a_tiles, targets, p_block = item
            fine_index = ((targets // PB) * CGROUPS + slot_group) * PB + targets % PB
            products = jnp.einsum('da,sdb->sab', p_block.astype(jnp.float32), a_tiles.astype(jnp.float32))
            return partial_sums.at[fine_index.astype(jnp.int32)].add(products), None

        zero_left = jnp.zeros((NB, coarse_width, BLOCK), jnp.float32)
        left_terms, _ = lax.scan(add_row, zero_left, (rows_a, rows_c, rows_p))
        left_half = lax.optimization_barrier(left_terms.astype(jnp.bfloat16))
        left_full = left_half.astype(jnp.float32).reshape(RGROUPS, ROW_BLOCKS, coarse_width, BLOCK)
        coarse_rows = jnp.einsum('gtad,gtdc->agc', left_full, p_full)
        return coarse_rows.reshape(coarse_width, NC * BLOCK)

    stacked = lax.map(group_rows, jnp.arange(RGROUPS, dtype=jnp.int32))
    return stacked.reshape(NC * BLOCK, NC * BLOCK)
```

```python
import functools

import jax
import jax.numpy as jnp
from jax import lax
from jax.experimental import pallas as pl
from jax.experimental.pallas import tpu as pltpu
from jax.sharding import PartitionSpec as P

MESH = pl.DeviceIdType.MESH
NX, NY, NZ = 4, 4, 8
T = 256
SLOTS = 4
ROWS = 16
NSLOT = ROWS * SLOTS
F32 = jnp.float32
BF16 = jnp.bfloat16


def place():
    row, col = lax.axis_index("row"), lax.axis_index("col")
    return row // NX, row % NX, col // 2, col % 2


def chain(a_cols):
    _, _, z, core = place()
    slot = lax.broadcasted_iota(jnp.int32, (1, NSLOT), 1)
    owner = slot // SLOTS
    dist = (owner // 2 - z + NZ) % NZ
    back = jnp.where(dist > NZ // 2, 1, 0)
    near = jnp.minimum(dist, NZ - dist)
    order = ((near * 2 + back) * 2 + (owner + core) % 2) * SLOTS + slot % SLOTS
    cols = a_cols.reshape(1, NSLOT)
    asked = jnp.concatenate([cols.reshape(NSLOT, 1), jnp.arange(16, dtype=jnp.int32).reshape(16, 1)], 0)
    before = jnp.concatenate([order.reshape(NSLOT, 1), jnp.full((16, 1), 1024, jnp.int32)], 0)
    hit = (cols == asked) & (order < before)
    best = jnp.max(jnp.where(hit, order * NSLOT + slot, -1), axis=1)
    return jnp.where(best < 0, NSLOT, best % NSLOT)


def kernel(link_ref, a_hbm, p_hbm, out_ref, run, a, pt, pc, xr, rcv, acc,
           load_sem, zs, zr, hs, hr, ws, wr, xs_sem, xr_sem, ss, sr):
    y, x, z, core = place()
    row, col = y * NX + x, z * 2 + core

    def zdev(step):
        return (row, ((z + step + NZ) % NZ) * 2 + core)

    def sibling():
        return (row, z * 2 + (1 - core))

    def xdev(step):
        return (y * NX + (x + step + NX) % NX, col)

    def ydev(step):
        return (((y + step + NY) % NY) * NX + x, col)

    load_p = [
        pltpu.make_async_copy(p_hbm.at[0, :, pl.ds(n * T, T)], pc.at[row, n], load_sem.at[n]) for n in range(2)
    ]
    for c in load_p:
        c.start()
    load_a = pltpu.make_async_copy(a_hbm, a, load_sem.at[2])
    load_a.start()

    barrier = pltpu.get_barrier_semaphore()
    partners = [zdev(1), zdev(-1), sibling(), xdev(1), xdev(-1), ydev(1), ydev(-1)]
    for dev in partners:
        pl.semaphore_signal(barrier, inc=1, device_id=dev, device_id_type=MESH)
    run[NSLOT] = jnp.zeros((2, T, T), F32)
    for n in range(2):
        load_p[n].wait()
        pt[col, n] = pc[row, n].T
    pl.semaphore_wait(barrier, len(partners))

    sends = []

    def copy(ref, send_sem, recv_sem, dev, dst=None):
        return pltpu.make_async_remote_copy(
            src_ref=ref, dst_ref=ref if dst is None else dst, send_sem=send_sem, recv_sem=recv_sem,
            device_id=dev, device_id_type=MESH,
        )

    def send(*args, **kw):
        c = copy(*args, **kw)
        c.start()
        sends.append(c)

    def zmsg(e, d, hop, recv):
        sign = 1 - 2 * d
        back = hop + 1 if recv else hop
        tile = ((z - sign * back + 2 * NZ) % NZ) * 2 + core
        ref = pt.at[tile, e] if hop < 3 else pt.at[tile, e, pl.ds(d * (T // 2), T // 2)]
        i = (e * 2 + d) * 4 + hop
        return ref, zs.at[i], zr.at[i], zdev(sign)

    def zsend(e, d, hop):
        send(*zmsg(e, d, hop, False))

    def zwait(e, d, hop):
        copy(*zmsg(e, d, hop, True)).wait_recv()

    def hmsg(e, shift, recv):
        tile = ((z + shift + NZ) % NZ) * 2 + ((1 - core) if recv else core)
        i = e * 8 + (shift + NZ) % NZ
        return pt.at[tile, e], hs.at[i], hr.at[i], sibling()

    def hsend(e, shift):
        send(*hmsg(e, shift, False))

    def hwait(e, shift):
        copy(*hmsg(e, shift, True)).wait_recv()

    names = {}

    def wid(name):
        return names.setdefault(name, len(names))

    def wmsg(name, dy, dx, part, dev):
        tile = ((y + dy + 2 * NY) % NY) * NX + (x + dx + 2 * NX) % NX
        ref = pc.at[tile]
        if part is not None:
            n, q = part
            ref = ref.at[n] if q is None else ref.at[n, pl.ds(q * (T // 2), T // 2)]
        i = wid(name)
        return ref, ws.at[i], wr.at[i], dev

    def step_of(axis, amount):
        return (0, amount) if axis == 0 else (amount, 0)

    def wdev(axis, d):
        return xdev(1 - 2 * d) if axis == 0 else ydev(1 - 2 * d)

    def wgo(name, axis, d, offset, part, recv):
        dy, dx = offset
        if recv:
            sy, sx = step_of(axis, -(1 - 2 * d))
            dy, dx = dy + sy, dx + sx
        m = wmsg(name, dy, dx, part, wdev(axis, d))
        if recv:
            copy(*m).wait_recv()
        else:
            send(*m)

    def w_own(axis, d, recv):
        wgo(("own", axis, d), axis, d, (0, 0), None, recv)

    def w_line2(axis, d, n, recv):
        wgo(("line2", axis, d, n), axis, d, step_of(axis, -(1 - 2 * d)), (n, d), recv)

    def w_diag(axis, d, o, recv):
        wgo(("diag", axis, d, o), axis, d, step_of(1 - axis, o), (1 - axis, None), recv)

    def w_diag2(axis, d, o, recv):
        ay, ax = step_of(axis, -(1 - 2 * d))
        by, bx = step_of(1 - axis, o)
        wgo(("diag2", axis, d, o), axis, d, (ay + by, ax + bx), (1 - axis, d), recv)

    both = [(axis, d) for axis in range(2) for d in range(2)]

    def left(dist, tiles):
        @pl.loop(0, tiles * SLOTS)
        def _(q):
            m = q // SLOTS
            tile = ((z + dist * (1 - 2 * (m // 2)) + NZ) % NZ) * 2 + (core + m) % 2
            s = tile * SLOTS + q % SLOTS
            prev = link_ref[s]
            for e in range(2):
                run[s, e] = run[prev, e] + jnp.dot(pt[tile, e], a[s], preferred_element_type=F32)

    for e in range(2):
        for d in range(2):
            zsend(e, d, 0)
        hsend(e, 0)
    for axis, d in both:
        w_own(axis, d, False)
    for e in range(2):
        for d in range(2):
            zwait(e, d, 0)
            zsend(e, d, 1)
        for d in range(2):
            hsend(e, -(1 - 2 * d))
    load_a.wait()
    for axis, d in both:
        w_own(axis, d, True)
    for axis, d in both:
        for n in range(2):
            w_line2(axis, d, n, False)
    for o in (-1, 1):
        for axis, d in both:
            w_diag(axis, d, o, False)
    for e in range(2):
        hwait(e, 0)
    left(0, 2)
    for e in range(2):
        for d in range(2):
            zwait(e, d, 1)
            zsend(e, d, 2)
        for d in range(2):
            hsend(e, -2 * (1 - 2 * d))
    for e in range(2):
        for d in range(2):
            hwait(e, 1 - 2 * d)
    left(1, 4)
    for axis, d in both:
        for n in range(2):
            w_line2(axis, d, n, True)
    for axis, d in both:
        w_diag(axis, d, 2, False)
    for e in range(2):
        for d in range(2):
            zwait(e, d, 2)
            zsend(e, d, 3)
        for d in range(2):
            hsend(e, -3 * (1 - 2 * d))
    for o in (-1, 1):
        for axis, d in both:
            w_diag(axis, d, o, True)
            w_diag2(axis, d, o, False)
    for e in range(2):
        for d in range(2):
            hwait(e, 2 * (1 - 2 * d))
    left(2, 4)
    for axis, d in both:
        w_diag(axis, d, 2, True)
        w_diag2(axis, d, 2, False)
    for e in range(2):
        for d in range(2):
            hwait(e, 3 * (1 - 2 * d))
    left(3, 4)
    for e in range(2):
        for d in range(2):
            zwait(e, d, 3)
        hsend(e, 4)
    for o in (-1, 1, 2):
        for axis, d in both:
            w_diag2(axis, d, o, True)
    for e in range(2):
        hwait(e, 4)
    left(4, 2)

    def product(block, q):
        last = link_ref[NSLOT + block]
        lhs = run[last, q % 2].astype(BF16)
        return jnp.dot(lhs, pc[block, q // 2], preferred_element_type=F32)

    def block_of(shift, k):
        return ((z + shift + NZ) % NZ) * 2 + k

    def exchange(shift):
        block = block_of(shift, 1 - core)
        m = (shift + NZ) % NZ
        base = m * 4

        @pl.loop(0, 4)
        def _(q):
            a[base + q] = product(block, q).astype(BF16)

        send(a.at[pl.ds(base, 4)], xs_sem.at[m], xr_sem.at[m], sibling(), dst=xr.at[pl.ds(base, 4)])

    def exchange_wait(shift):
        m = (shift + NZ) % NZ
        ref = xr.at[pl.ds(m * 4, 4)]
        copy(ref, xs_sem.at[m], xr_sem.at[m], sibling()).wait_recv()

    def own(shift, d):
        block = block_of(shift, core)
        m = (shift + NZ) % NZ
        exchange_wait(shift)

        @pl.loop(0, 4)
        def _(q):
            acc[d * 4 + q] = product(block, q) + xr[m * 4 + q].astype(F32)

    def rsend(d, hop, q):
        i = (d * 4 + hop) * 4 + q
        send(a.at[32 + i], ss.at[i], sr.at[i], zdev(1 - 2 * d), dst=rcv.at[i])

    def rwait(d, hop, q):
        i = (d * 4 + hop) * 4 + q
        copy(rcv.at[i], ss.at[i], sr.at[i], zdev(1 - 2 * d)).wait_recv()
        return rcv[i].astype(F32)

    exchange(4)
    exchange(3)
    exchange(-3)
    own(4, 0)
    for q in range(2):
        for d in range(2):
            t = 2 * d + q
            a[32 + d * 16 + t] = acc[t].astype(BF16)
            rsend(d, 0, t)
    for shift in (2, -2, 1, -1, 0):
        exchange(shift)
    for hop in range(1, 4):
        for d in range(2):
            own((4 - hop) * (1 - 2 * d), d)
        for step in range(4):
            for d in range(2):
                q = (2 + step) % 4 if d == 0 else step
                total = acc[d * 4 + q]
                if hop > 1 or step >= 2:
                    total = total + rwait(d, hop - 1, q)
                a[32 + (d * 4 + hop) * 4 + q] = total.astype(BF16)
                rsend(d, hop, q)
    own(0, 0)
    for step in range(4):
        for d in range(2):
            q = (2 + step) % 4 if d == 0 else step
            acc[q] = acc[q] + rwait(d, 3, q)
    for q in range(4):
        out_ref[pl.ds((q % 2) * T, T), pl.ds((q // 2) * T, T)] = acc[q]
    for c in sends:
        c.wait_send()


def per_device(a_vals, a_cols, p_vals):
    links = chain(a_cols)
    dma = pltpu.SemaphoreType.DMA
    return pl.pallas_call(
        kernel,
        out_shape=jax.ShapeDtypeStruct((2 * T, 2 * T), F32),
        in_specs=[
            pl.BlockSpec(memory_space=pltpu.SMEM),
            pl.BlockSpec(memory_space=pl.ANY),
            pl.BlockSpec(memory_space=pl.ANY),
        ],
        out_specs=pl.BlockSpec(memory_space=pltpu.VMEM),
        scratch_shapes=[
            pltpu.VMEM((NSLOT + 1, 2, T, T), F32),
            pltpu.VMEM((NSLOT, T, T), BF16),
            pltpu.VMEM((ROWS, 2, T, T), BF16),
            pltpu.VMEM((ROWS, 2, T, T), BF16),
            pltpu.VMEM((32, T, T), BF16),
            pltpu.VMEM((32, T, T), BF16),
            pltpu.VMEM((8, T, T), F32),
            dma((3,)),
            dma((16,)), dma((16,)),
            dma((16,)), dma((16,)),
            dma((36,)), dma((36,)),
            dma((8,)), dma((8,)),
            dma((32,)), dma((32,)),
        ],
        compiler_params=pltpu.CompilerParams(
            collective_id=0, has_side_effects=True, vmem_limit_bytes=62 * 1024 * 1024
        ),
        cost_estimate=pl.CostEstimate(flops=6_442_450_944, bytes_accessed=10_000_000, transcendentals=0),
    )(links, a_vals.reshape(NSLOT, T, T), p_vals)


def solution(mesh):
    return jax.shard_map(
        per_device,
        mesh=mesh,
        in_specs=(P("row", "col", None, None), P("row", "col"), P(("row", "col"), None, None)),
        out_specs=P("row", "col"),
        check_vma=False,
    )
```

```python
import functools

import jax
import jax.numpy as jnp
from jax import lax
from jax.experimental import pallas as pl
from jax.experimental.pallas import tpu as pltpu
from jax.sharding import PartitionSpec as P

MESH = pl.DeviceIdType.MESH
NX, NY, NZ = 4, 4, 8
T = 256
SLOTS = 4
ROWS = 16
NSLOT = ROWS * SLOTS
HALF, QUART = T // 2, T // 4
UNITS = ((0, 0), (1, 0), (0, 1), (1, 1))
F32 = jnp.float32
BF16 = jnp.bfloat16


def place():
    row, col = lax.axis_index("row"), lax.axis_index("col")
    return row // NX, row % NX, col // 2, col % 2


def chain(cols_ref, links_ref, z, core):
    def order_of(owner, k):
        dist = (owner // 2 - z + NZ) % NZ
        back = jnp.where(dist > NZ // 2, 1, 0)
        near = jnp.minimum(dist, NZ - dist)
        return ((near * 2 + back) * 2 + (owner + core) % 2) * SLOTS + k

    shape = (ROWS, ROWS)
    down = lax.broadcasted_iota(jnp.int32, shape, 0)
    across = lax.broadcasted_iota(jnp.int32, shape, 1)
    turned = [jnp.broadcast_to(cols_ref[k:k + 1, :], shape) for k in range(SLOTS)]
    cols = [jnp.broadcast_to(jnp.sum(jnp.where(down == across, c, 0), axis=1, keepdims=True), shape) for c in turned]
    for k in range(SLOTS + 1):
        asked = cols[k] if k < SLOTS else down
        before = order_of(down, k) if k < SLOTS else jnp.full(shape, 1024, jnp.int32)
        best = jnp.full(shape, -1, jnp.int32)
        for j in range(SLOTS):
            order = order_of(across, j)
            hit = (turned[j] == asked) & (order < before)
            best = jnp.maximum(best, jnp.where(hit, order * NSLOT + across * SLOTS + j, -1))
        best = jnp.max(best, axis=1, keepdims=True)
        links_ref[:, k:k + 1] = jnp.where(best < 0, NSLOT, best % NSLOT)


def kernel(cols_hbm, a_hbm, p_hbm, out_hbm, out_ref, run, a, pt, pc, xr, rcv, first, acc, cols, links, link_ref,
           load_sem, out_sem, zs, zr, hs, hr, ws, wr, xs_sem, xr_sem, ss, sr):
    y, x, z, core = place()
    row, col = y * NX + x, z * 2 + core

    def zdev(step):
        return (row, ((z + step + NZ) % NZ) * 2 + core)

    def sibling():
        return (row, z * 2 + (1 - core))

    def xdev(step):
        return (y * NX + (x + step + NX) % NX, col)

    def ydev(step):
        return (((y + step + NY) % NY) * NX + x, col)

    load_p = [
        pltpu.make_async_copy(p_hbm.at[0, :, pl.ds(n * T, T)], pc.at[n, row], load_sem.at[n]) for n in range(2)
    ]
    for c in load_p:
        c.start()
    load_cols = pltpu.make_async_copy(cols_hbm, cols, load_sem.at[3])
    load_cols.start()
    load_a = pltpu.make_async_copy(a_hbm, a, load_sem.at[2])
    load_a.start()

    barrier = pltpu.get_barrier_semaphore()
    partners = [zdev(1), zdev(-1), sibling(), xdev(1), xdev(-1), ydev(1), ydev(-1)]
    for dev in partners:
        pl.semaphore_signal(barrier, inc=1, device_id=dev, device_id_type=MESH)
    for e in range(2):
        run[e, NSLOT] = jnp.zeros((T, T), F32)
        load_p[e].wait()
        pt[e, col] = pc[e, row].T
    pl.semaphore_wait(barrier, len(partners))

    result = []
    late = []
    held = ([], [])

    def copy(ref, send_sem, recv_sem, dev, dst=None):
        return pltpu.make_async_remote_copy(
            src_ref=ref, dst_ref=ref if dst is None else dst, send_sem=send_sem, recv_sem=recv_sem,
            device_id=dev, device_id_type=MESH,
        )

    def send(into, *args, **kw):
        c = copy(*args, **kw)
        c.start()
        into.append(c)

    def zmsg(e, d, hop, q, recv):
        sign = 1 - 2 * d
        back = hop + 1 if recv else hop
        tile = ((z - sign * back + 2 * NZ) % NZ) * 2 + core
        i = ((e * 2 + d) * 4 + hop) * 2 + q
        return pt.at[e, tile, pl.ds(q * HALF, HALF)], zs.at[i], zr.at[i], zdev(sign)

    def zsend(e, hop, k):
        for d in range(2):
            send(held[e], *zmsg(e, d, hop, (d + k) % 2, False))

    def zwait(e, hop, k):
        for d in range(2):
            copy(*zmsg(e, d, hop, (d + k) % 2, True)).wait_recv()

    def hmsg(e, shift, recv):
        tile = ((z + shift + NZ) % NZ) * 2 + ((1 - core) if recv else core)
        i = e * 8 + (shift + NZ) % NZ
        return pt.at[e, tile], hs.at[i], hr.at[i], sibling()

    def hsend(e, *shifts):
        for shift in shifts:
            send(held[e], *hmsg(e, shift, False))

    def hwait(e, *shifts):
        for shift in shifts:
            copy(*hmsg(e, shift, True)).wait_recv()

    names = {}

    def step_of(axis, amount):
        return (0, amount) if axis == 0 else (amount, 0)

    def wgo(name, axis, d, offset, rows, recv):
        sign = 1 - 2 * d
        dy, dx = offset
        if recv:
            sy, sx = step_of(axis, -sign)
            dy, dx = dy + sy, dx + sx
        tile = ((y + dy + 2 * NY) % NY) * NX + (x + dx + 2 * NX) % NX
        ref = pc.at[name[0], tile]
        if rows is not None:
            ref = ref.at[pl.ds(*rows)]
        i = names.setdefault((axis, d) + name, len(names))
        m = (ref, ws.at[i], wr.at[i], xdev(sign) if axis == 0 else ydev(sign))
        if recv:
            copy(*m).wait_recv()
        else:
            send(late, *m)

    both = [(axis, d) for axis in range(2) for d in range(2)]

    def w_own(n, recv):
        for axis, d in both:
            wgo((n, "own"), axis, d, (0, 0), None, recv)

    def w_line2(n, recv):
        for axis, d in both:
            for f in range(2):
                wgo((n, "line2", f), axis, d, step_of(axis, 2 * d - 1), (f * HALF + d * QUART, QUART), recv)

    def w_diag(n, o, recv):
        for axis, d in both:
            wgo((n, "diag", o), axis, d, step_of(1 - axis, o), ((1 - axis) * HALF, HALF), recv)

    def w_diag2(n, o, recv):
        for axis, d in both:
            ay, ax = step_of(axis, 2 * d - 1)
            by, bx = step_of(1 - axis, o)
            wgo((n, "diag2", o), axis, d, (ay + by, ax + bx), ((1 - axis) * HALF + d * QUART, QUART), recv)

    def left(e, dist, lo, hi):
        @pl.loop(lo, hi)
        def _(m):
            tile = ((z + dist * (1 - 2 * (m // 2)) + NZ) % NZ) * 2 + (core + m) % 2
            for k in range(SLOTS):
                s = tile * SLOTS + k
                prev = link_ref[tile, k]
                run[e, s] = run[e, prev] + jnp.dot(pt[e, tile], a[s], preferred_element_type=F32)

    def product(e, n, block):
        last = link_ref[block, SLOTS]
        return jnp.dot(run[e, last].astype(BF16), pc[n, block], preferred_element_type=F32)

    def block_of(shift, k):
        return ((z + shift + NZ) % NZ) * 2 + k

    def xmsg(u, shift):
        m = (shift + NZ) % NZ
        e, n = UNITS[u]
        i = u * 8 + m
        return pt.at[e, n * 8 + m], xs_sem.at[i], xr_sem.at[i], sibling(), xr.at[i]

    def exchange(u, *shifts):
        e, n = UNITS[u]
        for shift in shifts:
            pt[e, n * 8 + (shift + NZ) % NZ] = product(e, n, block_of(shift, 1 - core)).astype(BF16)
            send(late, *xmsg(u, shift))

    def own(u, shift):
        e, n = UNITS[u]
        value = product(e, n, block_of(shift, core))
        copy(*xmsg(u, shift)).wait_recv()
        return value + xr[u * 8 + (shift + NZ) % NZ].astype(F32)

    def rmsg(u, d, hop, r):
        i = (u * 2 + d) * 4 + hop
        buf = first.at[i] if u == 0 else a.at[i - 8]
        rows = pl.ds(r * HALF, HALF)
        return buf.at[rows], ss.at[i * 2 + r], sr.at[i * 2 + r], zdev(1 - 2 * d), rcv.at[i, rows]

    def pass_on(u, d, hop, r, value):
        m = rmsg(u, d, hop, r)
        m[0][...] = value.astype(BF16)
        send(late, *m)

    def arrived(u, d, hop, r):
        copy(*rmsg(u, d, hop, r)).wait_recv()
        return rcv[(u * 2 + d) * 4 + hop, pl.ds(r * HALF, HALF)].astype(F32)

    def ring(u, step):
        e, n = UNITS[u]
        slot = u * 2
        hop = (step + 1) // 2
        if step == 0:
            total = own(u, 4)
            for d in range(2):
                pass_on(u, d, 0, d, total[d * HALF:(d + 1) * HALF])
            return
        if step == 7:
            out_ref[pl.ds(e * T, T), pl.ds(n * T, T)] = own(u, 0)
        elif step % 2 == 1:
            for d in range(2):
                acc[slot + d] = own(u, (4 - hop) * (1 - 2 * d))
        for d in range(2):
            r = 1 - d if step % 2 == 1 else d
            if step >= 7:
                rows = pl.ds(e * T + r * HALF, HALF), pl.ds(n * T, T)
                out_ref[rows] = out_ref[rows] + arrived(u, d, 3, r)
                continue
            total = acc[slot + d, pl.ds(r * HALF, HALF)]
            if step > 1:
                total = total + arrived(u, d, hop - 1, r)
            pass_on(u, d, hop, r, total)
        if step == 8:
            tile = pl.ds(e * T, T), pl.ds(n * T, T)
            result.append(pltpu.make_async_copy(out_ref.at[tile], out_hbm.at[tile], out_sem.at[u]))
            result[-1].start()

    zsend(0, 0, 0)
    zsend(0, 0, 1)
    hsend(0, 0)
    w_own(0, False)
    zsend(1, 0, 0)
    zsend(1, 0, 1)
    hsend(1, 0)
    load_cols.wait()
    chain(cols, links, z, core)
    to_scalars = pltpu.make_async_copy(links, link_ref, load_sem.at[4])
    to_scalars.start()
    load_a.wait()
    to_scalars.wait()
    zwait(0, 0, 0)
    zsend(0, 1, 0)
    zwait(0, 0, 1)
    zsend(0, 1, 1)
    hsend(0, 1, -1)
    w_own(0, True)
    w_line2(0, False)
    w_diag(0, -1, False)
    w_diag(0, 1, False)
    zwait(1, 0, 0)
    zsend(1, 1, 0)
    zwait(1, 0, 1)
    zsend(1, 1, 1)
    hsend(1, 1, -1)
    hwait(0, 0)
    left(0, 0, 0, 2)
    hwait(1, 0)
    left(1, 0, 0, 2)
    zwait(0, 1, 0)
    zsend(0, 2, 0)
    zwait(0, 1, 1)
    zsend(0, 2, 1)
    hsend(0, 2, -2)
    w_line2(0, True)
    w_diag(0, 2, False)
    w_own(1, False)
    hwait(0, 1, -1)
    left(0, 1, 0, 4)
    zwait(1, 1, 0)
    zsend(1, 2, 0)
    zwait(1, 1, 1)
    zsend(1, 2, 1)
    hsend(1, 2, -2)
    w_diag(0, -1, True)
    w_diag(0, 1, True)
    w_diag2(0, -1, False)
    w_diag2(0, 1, False)
    hwait(1, 1, -1)
    left(1, 1, 0, 4)
    zwait(0, 2, 0)
    zsend(0, 3, 0)
    w_diag(0, 2, True)
    w_diag2(0, 2, False)
    zwait(0, 2, 1)
    hsend(0, 3, -3)
    hwait(0, 2, -2)
    left(0, 2, 0, 4)
    zwait(1, 2, 0)
    zsend(1, 3, 0)
    zwait(1, 2, 1)
    hsend(1, 3, -3)
    hwait(0, 3, -3)
    left(0, 3, 0, 4)
    zwait(0, 3, 0)
    hsend(0, 4)
    left(0, 4, 0, 1)
    w_diag2(0, -1, True)
    w_diag2(0, 1, True)
    w_diag2(0, 2, True)
    hwait(0, 4)
    left(0, 4, 1, 2)
    for c in held[0]:
        c.wait_send()
    exchange(0, 4, 3, -3)
    hwait(1, 2, -2)
    left(1, 2, 0, 4)
    ring(0, 0)
    ring(0, 1)
    zwait(1, 3, 0)
    hsend(1, 4)
    hwait(1, 3, -3)
    left(1, 3, 0, 4)
    left(1, 4, 0, 1)
    hwait(1, 4)
    left(1, 4, 1, 2)
    for c in held[1]:
        c.wait_send()
    exchange(1, 4, 3, -3)
    w_own(1, True)
    w_line2(1, False)
    w_diag(1, -1, False)
    w_diag(1, 1, False)
    exchange(0, 2, -2)
    ring(1, 0)
    ring(1, 1)
    ring(0, 2)
    ring(0, 3)
    exchange(1, 2, -2)
    w_line2(1, True)
    w_diag(1, 2, False)
    exchange(0, 1, -1)
    ring(1, 2)
    ring(1, 3)
    w_diag(1, -1, True)
    w_diag(1, 1, True)
    w_diag2(1, -1, False)
    w_diag2(1, 1, False)
    ring(0, 4)
    w_diag(1, 2, True)
    w_diag2(1, 2, False)
    exchange(1, 1, -1)
    ring(0, 5)
    ring(0, 6)
    w_diag2(1, -1, True)
    w_diag2(1, 1, True)
    w_diag2(1, 2, True)

    exchange(2, 4, 3, -3)
    ring(1, 4)
    ring(2, 0)
    exchange(3, 4, 3, -3)
    ring(2, 1)
    exchange(2, 2, -2)
    ring(3, 0)
    ring(3, 1)
    exchange(3, 2, -2)
    ring(1, 5)
    exchange(0, 0)
    ring(2, 2)
    ring(3, 2)
    exchange(2, 1, -1)
    ring(1, 6)
    ring(2, 3)
    exchange(3, 1, -1)
    ring(3, 3)
    exchange(1, 0)
    ring(0, 7)
    ring(0, 8)
    exchange(2, 0)
    ring(2, 4)
    ring(3, 4)
    exchange(3, 0)
    ring(2, 5)
    ring(3, 5)
    ring(1, 7)
    ring(1, 8)
    ring(2, 6)
    ring(3, 6)
    ring(2, 7)
    ring(3, 7)
    ring(2, 8)
    ring(3, 8)
    for c in late:
        c.wait_send()
    for c in result:
        c.wait()


def per_device(a_vals, a_cols, p_vals):
    dma = pltpu.SemaphoreType.DMA
    return pl.pallas_call(
        kernel,
        out_shape=jax.ShapeDtypeStruct((2 * T, 2 * T), F32),
        in_specs=[
            pl.BlockSpec(memory_space=pl.ANY),
            pl.BlockSpec(memory_space=pl.ANY),
            pl.BlockSpec(memory_space=pl.ANY),
        ],
        out_specs=pl.BlockSpec(memory_space=pl.ANY),
        scratch_shapes=[
            pltpu.VMEM((2 * T, 2 * T), F32),
            pltpu.VMEM((2, NSLOT + 1, T, T), F32),
            pltpu.VMEM((NSLOT, T, T), BF16),
            pltpu.VMEM((2, ROWS, T, T), BF16),
            pltpu.VMEM((2, ROWS, T, T), BF16),
            pltpu.VMEM((32, T, T), BF16),
            pltpu.VMEM((32, T, T), BF16),
            pltpu.VMEM((8, T, T), BF16),
            pltpu.VMEM((8, T, T), F32),
            pltpu.VMEM((SLOTS, ROWS), jnp.int32),
            pltpu.VMEM((ROWS, 128), jnp.int32),
            pltpu.SMEM((ROWS, 128), jnp.int32),
            dma((5,)), dma((4,)),
            dma((32,)), dma((32,)),
            dma((16,)), dma((16,)),
            dma((72,)), dma((72,)),
            dma((32,)), dma((32,)),
            dma((64,)), dma((64,)),
        ],
        compiler_params=pltpu.CompilerParams(
            collective_id=0, has_side_effects=True, vmem_limit_bytes=62 * 1024 * 1024
        ),
        cost_estimate=pl.CostEstimate(flops=6_442_450_944, bytes_accessed=10_000_000, transcendentals=0),
    )(a_cols.T, a_vals.reshape(NSLOT, T, T), p_vals)


def solution(mesh):
    return jax.shard_map(
        per_device,
        mesh=mesh,
        in_specs=(P("row", "col", None, None), P("row", "col"), P(("row", "col"), None, None)),
        out_specs=P("row", "col"),
        check_vma=False,
    )
```

```python
import functools

import jax
import jax.numpy as jnp
from jax import lax
from jax.experimental import pallas as pl
from jax.experimental.pallas import tpu as pltpu
from jax.sharding import PartitionSpec as P

MESH = pl.DeviceIdType.MESH
NX, NY, NZ = 4, 4, 8
T = 256
SLOTS = 4
ROWS = 16
NSLOT = ROWS * SLOTS
HALF, QUART = T // 2, T // 4
UNITS = ((0, 0), (1, 0), (0, 1), (1, 1))
F32 = jnp.float32
BF16 = jnp.bfloat16


def place():
    row, col = lax.axis_index("row"), lax.axis_index("col")
    return row // NX, row % NX, col // 2, col % 2


def chain(cols_ref, links_ref, z, core):
    def order_of(owner, k):
        dist = (owner // 2 - z + NZ) % NZ
        back = jnp.where(dist > NZ // 2, 1, 0)
        near = jnp.minimum(dist, NZ - dist)
        return ((near * 2 + back) * 2 + (owner + core) % 2) * SLOTS + k

    shape = (ROWS, ROWS)
    down = lax.broadcasted_iota(jnp.int32, shape, 0)
    across = lax.broadcasted_iota(jnp.int32, shape, 1)
    turned = [jnp.broadcast_to(cols_ref[k:k + 1, :], shape) for k in range(SLOTS)]
    cols = [jnp.broadcast_to(jnp.sum(jnp.where(down == across, c, 0), axis=1, keepdims=True), shape) for c in turned]
    for k in range(SLOTS + 1):
        asked = cols[k] if k < SLOTS else down
        before = order_of(down, k) if k < SLOTS else jnp.full(shape, 1024, jnp.int32)
        best = jnp.full(shape, -1, jnp.int32)
        for j in range(SLOTS):
            order = order_of(across, j)
            hit = (turned[j] == asked) & (order < before)
            best = jnp.maximum(best, jnp.where(hit, order * NSLOT + across * SLOTS + j, -1))
        best = jnp.max(best, axis=1, keepdims=True)
        links_ref[:, k:k + 1] = jnp.where(best < 0, NSLOT, best % NSLOT)


def kernel(cols_hbm, a_hbm, p_hbm, out_hbm, out_ref, run, a, pt, pc, xr, rcv, first, acc, cols, links, link_ref,
           load_sem, out_sem, zs, zr, hs, hr, ws, wr, xs_sem, xr_sem, ss, sr):
    y, x, z, core = place()
    row, col = y * NX + x, z * 2 + core

    def zdev(step):
        return (row, ((z + step + NZ) % NZ) * 2 + core)

    def sibling():
        return (row, z * 2 + (1 - core))

    def xdev(step):
        return (y * NX + (x + step + NX) % NX, col)

    def ydev(step):
        return (((y + step + NY) % NY) * NX + x, col)

    load_p = [
        pltpu.make_async_copy(p_hbm.at[0, pl.ds((f * 2 + q) * QUART, QUART), pl.ds(n * T, T)], pc.at[n, y, x, f, q], load_sem.at[(n * 2 + f) * 2 + q])
        for n in range(2) for f in range(2) for q in range(2)
    ]
    for c in load_p:
        c.start()
    load_cols = pltpu.make_async_copy(cols_hbm, cols, load_sem.at[9])
    load_cols.start()
    load_a = pltpu.make_async_copy(a_hbm, a, load_sem.at[8])
    load_a.start()

    barrier = pltpu.get_barrier_semaphore()
    partners = [zdev(1), zdev(-1), sibling(), xdev(1), xdev(-1), ydev(1), ydev(-1)]
    for dev in partners:
        pl.semaphore_signal(barrier, inc=1, device_id=dev, device_id_type=MESH)
    for e in range(2):
        run[e, NSLOT] = jnp.zeros((T, T), F32)
        for c in load_p[4 * e:4 * e + 4]:
            c.wait()
        pt[e, col] = pc[e, y, x].reshape(T, T).T
    pl.semaphore_wait(barrier, len(partners))

    result = []
    late = []
    held = ([], [])

    def copy(ref, send_sem, recv_sem, dev, dst=None):
        return pltpu.make_async_remote_copy(
            src_ref=ref, dst_ref=ref if dst is None else dst, send_sem=send_sem, recv_sem=recv_sem,
            device_id=dev, device_id_type=MESH,
        )

    def send(into, *args, **kw):
        c = copy(*args, **kw)
        c.start()
        into.append(c)

    def drain(keep):
        while len(late) > keep:
            late.pop(0).wait_send()

    def zmsg(e, d, hop, q, recv):
        sign = 1 - 2 * d
        back = hop + 1 if recv else hop
        tile = ((z - sign * back + 2 * NZ) % NZ) * 2 + core
        i = ((e * 2 + d) * 4 + hop) * 2 + q
        return pt.at[e, tile, pl.ds(q * HALF, HALF)], zs.at[i], zr.at[i], zdev(sign)

    def zsend(e, hop, k):
        for d in range(2):
            send(held[e], *zmsg(e, d, hop, (d + k) % 2, False))

    def zwait(e, hop, k):
        for d in range(2):
            copy(*zmsg(e, d, hop, (d + k) % 2, True)).wait_recv()

    def hmsg(e, shift, recv):
        tile = ((z + shift + NZ) % NZ) * 2 + ((1 - core) if recv else core)
        i = e * 8 + (shift + NZ) % NZ
        return pt.at[e, tile], hs.at[i], hr.at[i], sibling()

    def hsend(e, *shifts):
        for shift in shifts:
            send(held[e], *hmsg(e, shift, False))

    def hwait(e, *shifts):
        for shift in shifts:
            copy(*hmsg(e, shift, True)).wait_recv()

    def wmsg(n, stage, axis, d, recv):
        sign = 1 - 2 * d
        back = (1 if stage % 2 == 0 else 2) if recv else stage % 2
        along = ((x if axis == 0 else y) - sign * back + 2 * NX) % NX
        across = slice(None) if stage >= 2 else (y if axis == 0 else x)
        half = axis if stage < 2 else 1 - axis
        ref = pc.at[n, across, along, half] if axis == 0 else pc.at[n, along, across, half]
        if stage % 2 == 1:
            ref = ref.at[d] if stage == 1 else ref.at[:, d]
        i = (stage * 2 + axis) * 2 + d
        return ref, ws.at[i], wr.at[i], xdev(sign) if axis == 0 else ydev(sign)

    def wsend(n, stage):
        for axis in range(2):
            for d in range(2):
                send(late, *wmsg(n, stage, axis, d, False))

    def wwait(n, stage):
        for axis in range(2):
            for d in range(2):
                copy(*wmsg(n, stage, axis, d, True)).wait_recv()

    names = {}

    def step_of(axis, amount):
        return (0, amount) if axis == 0 else (amount, 0)

    def wgo(name, axis, d, offset, part, recv):
        sign = 1 - 2 * d
        dy, dx = offset
        if recv:
            sy, sx = step_of(axis, -sign)
            dy, dx = dy + sy, dx + sx
        ref = pc.at[(0, (y + dy + 2 * NY) % NY, (x + dx + 2 * NX) % NX) + part]
        i = 16 + names.setdefault((axis, d) + name, len(names))
        m = (ref, ws.at[i], wr.at[i], xdev(sign) if axis == 0 else ydev(sign))
        if recv:
            copy(*m).wait_recv()
        else:
            send(late, *m)

    both = [(axis, d) for axis in range(2) for d in range(2)]

    def w_own(recv):
        for axis, d in both:
            wgo(("own",), axis, d, (0, 0), (), recv)

    def w_line2(recv):
        for axis, d in both:
            for f in range(2):
                wgo(("line2", f), axis, d, step_of(axis, 2 * d - 1), (f, d), recv)

    def w_diag(o, recv):
        for axis, d in both:
            wgo(("diag", o), axis, d, step_of(1 - axis, o), (1 - axis,), recv)

    def w_diag2(o, recv):
        for axis, d in both:
            ay, ax = step_of(axis, 2 * d - 1)
            by, bx = step_of(1 - axis, o)
            wgo(("diag2", o), axis, d, (ay + by, ax + bx), (1 - axis, d), recv)

    def left(e, dist, lo, hi):
        @pl.loop(lo, hi)
        def _(m):
            tile = ((z + dist * (1 - 2 * (m // 2)) + NZ) % NZ) * 2 + (core + m) % 2
            for k in range(SLOTS):
                s = tile * SLOTS + k
                prev = link_ref[tile, k]
                run[e, s] = run[e, prev] + jnp.dot(pt[e, tile], a[s], preferred_element_type=F32)

    def product(e, n, block):
        last = link_ref[block, SLOTS]
        return jnp.dot(run[e, last].astype(BF16), pc[n, block // NX, block % NX].reshape(T, T), preferred_element_type=F32)

    def block_of(shift, k):
        return ((z + shift + NZ) % NZ) * 2 + k

    def xmsg(u, shift):
        m = (shift + NZ) % NZ
        e, n = UNITS[u]
        i = u * 8 + m
        return pt.at[e, n * 8 + m], xs_sem.at[i], xr_sem.at[i], sibling(), xr.at[i]

    def exchange(u, *shifts):
        e, n = UNITS[u]
        for shift in shifts:
            pt[e, n * 8 + (shift + NZ) % NZ] = product(e, n, block_of(shift, 1 - core)).astype(BF16)
            send(late, *xmsg(u, shift))

    def own(u, shift):
        e, n = UNITS[u]
        value = product(e, n, block_of(shift, core))
        copy(*xmsg(u, shift)).wait_recv()
        return value + xr[u * 8 + (shift + NZ) % NZ].astype(F32)

    def rmsg(u, d, hop, r):
        i = (u * 2 + d) * 4 + hop
        buf = first.at[i] if u == 0 else a.at[i - 8]
        rows = pl.ds(r * HALF, HALF)
        return buf.at[rows], ss.at[i * 2 + r], sr.at[i * 2 + r], zdev(1 - 2 * d), rcv.at[i, rows]

    def pass_on(u, d, hop, r, value):
        m = rmsg(u, d, hop, r)
        m[0][...] = value.astype(BF16)
        send(late, *m)

    def arrived(u, d, hop, r):
        copy(*rmsg(u, d, hop, r)).wait_recv()
        return rcv[(u * 2 + d) * 4 + hop, pl.ds(r * HALF, HALF)].astype(F32)

    def ring(u, step):
        e, n = UNITS[u]
        slot = u * 2
        hop = (step + 1) // 2
        if step == 0:
            total = own(u, 4)
            for d in range(2):
                pass_on(u, d, 0, d, total[d * HALF:(d + 1) * HALF])
            return
        if step == 7:
            out_ref[pl.ds(e * T, T), pl.ds(n * T, T)] = own(u, 0)
        elif step % 2 == 1:
            for d in range(2):
                acc[slot + d] = own(u, (4 - hop) * (1 - 2 * d))
        for d in range(2):
            r = 1 - d if step % 2 == 1 else d
            if step >= 7:
                rows = pl.ds(e * T + r * HALF, HALF), pl.ds(n * T, T)
                out_ref[rows] = out_ref[rows] + arrived(u, d, 3, r)
                continue
            total = acc[slot + d, pl.ds(r * HALF, HALF)]
            if step > 1:
                total = total + arrived(u, d, hop - 1, r)
            pass_on(u, d, hop, r, total)
        if step == 8:
            tile = pl.ds(e * T, T), pl.ds(n * T, T)
            result.append(pltpu.make_async_copy(out_ref.at[tile], out_hbm.at[tile], out_sem.at[u]))
            result[-1].start()

    zsend(0, 0, 0)
    zsend(0, 0, 1)
    hsend(0, 0)
    w_own(False)
    zsend(1, 0, 0)
    zsend(1, 0, 1)
    hsend(1, 0)
    load_cols.wait()
    chain(cols, links, z, core)
    to_scalars = pltpu.make_async_copy(links, link_ref, load_sem.at[10])
    to_scalars.start()
    load_a.wait()
    to_scalars.wait()
    hwait(0, 0)
    left(0, 0, 0, 2)
    zwait(0, 0, 0)
    zsend(0, 1, 0)
    zwait(0, 0, 1)
    zsend(0, 1, 1)
    hsend(0, 1, -1)
    w_own(True)
    w_line2(False)
    w_diag(-1, False)
    w_diag(1, False)
    zwait(1, 0, 0)
    zsend(1, 1, 0)
    zwait(1, 0, 1)
    zsend(1, 1, 1)
    hsend(1, 1, -1)
    hwait(0, 1, -1)
    left(0, 1, 0, 4)
    hwait(1, 0)
    left(1, 0, 0, 2)
    zwait(0, 1, 0)
    zsend(0, 2, 0)
    zwait(0, 1, 1)
    zsend(0, 2, 1)
    hsend(0, 2, -2)
    w_line2(True)
    w_diag(2, False)
    wsend(1, 0)
    hwait(1, 1, -1)
    left(1, 1, 0, 4)
    zwait(1, 1, 0)
    zsend(1, 2, 0)
    zwait(1, 1, 1)
    zsend(1, 2, 1)
    hsend(1, 2, -2)
    w_diag(-1, True)
    w_diag(1, True)
    w_diag2(-1, False)
    w_diag2(1, False)
    hwait(0, 2, -2)
    left(0, 2, 0, 4)
    zwait(0, 2, 0)
    zsend(0, 3, 0)
    zwait(0, 2, 1)
    hsend(0, 3, -3)
    w_diag(2, True)
    w_diag2(2, False)
    wwait(1, 0)
    wsend(1, 1)
    hwait(1, 2, -2)
    left(1, 2, 0, 4)
    hwait(0, 3, -3)
    left(0, 3, 0, 4)
    zwait(1, 2, 0)
    zsend(1, 3, 0)
    zwait(1, 2, 1)
    hsend(1, 3, -3)
    zwait(0, 3, 0)
    hsend(0, 4)
    left(0, 4, 0, 1)
    hwait(0, 4)
    left(0, 4, 1, 2)
    for c in held[0]:
        c.wait_send()
    w_diag2(-1, True)
    w_diag2(1, True)
    w_diag2(2, True)
    exchange(0, 4, 3, -3)
    hwait(1, 3, -3)
    left(1, 3, 0, 2)
    ring(0, 0)
    ring(0, 1)
    wwait(1, 1)
    wsend(1, 2)
    zwait(1, 3, 0)
    hsend(1, 4)
    left(1, 3, 2, 4)
    left(1, 4, 0, 1)
    hwait(1, 4)
    left(1, 4, 1, 2)
    for c in held[1]:
        c.wait_send()
    exchange(1, 4, 3, -3)

    exchange(0, 2, -2)
    ring(1, 0)
    ring(1, 1)
    ring(0, 2)
    ring(0, 3)
    exchange(1, 2, -2)
    exchange(0, 1, -1)
    ring(1, 2)
    ring(1, 3)
    wwait(1, 2)
    wsend(1, 3)
    ring(0, 4)
    exchange(1, 1, -1)
    ring(0, 5)
    ring(0, 6)
    wwait(1, 3)

    exchange(2, 4, 3, -3)
    ring(1, 4)
    ring(2, 0)
    exchange(3, 4, 3, -3)
    ring(2, 1)
    exchange(2, 2, -2)
    ring(3, 0)
    ring(3, 1)
    exchange(3, 2, -2)
    ring(1, 5)
    exchange(0, 0)
    ring(2, 2)
    ring(3, 2)
    exchange(2, 1, -1)
    ring(1, 6)
    ring(2, 3)
    exchange(3, 1, -1)
    ring(3, 3)
    exchange(1, 0)
    ring(0, 7)
    ring(0, 8)
    exchange(2, 0)
    ring(2, 4)
    ring(3, 4)
    exchange(3, 0)
    ring(2, 5)
    ring(3, 5)
    ring(1, 7)
    ring(1, 8)
    ring(2, 6)
    ring(3, 6)
    ring(2, 7)
    ring(3, 7)
    ring(2, 8)
    ring(3, 8)
    drain(0)
    for c in result:
        c.wait()


def per_device(a_vals, a_cols, p_vals):
    dma = pltpu.SemaphoreType.DMA
    return pl.pallas_call(
        kernel,
        out_shape=jax.ShapeDtypeStruct((2 * T, 2 * T), F32),
        in_specs=[
            pl.BlockSpec(memory_space=pl.ANY),
            pl.BlockSpec(memory_space=pl.ANY),
            pl.BlockSpec(memory_space=pl.ANY),
        ],
        out_specs=pl.BlockSpec(memory_space=pl.ANY),
        scratch_shapes=[
            pltpu.VMEM((2 * T, 2 * T), F32),
            pltpu.VMEM((2, NSLOT + 1, T, T), F32),
            pltpu.VMEM((NSLOT, T, T), BF16),
            pltpu.VMEM((2, ROWS, T, T), BF16),
            pltpu.VMEM((2, NY, NX, 2, 2, QUART, T), BF16),
            pltpu.VMEM((32, T, T), BF16),
            pltpu.VMEM((32, T, T), BF16),
            pltpu.VMEM((8, T, T), BF16),
            pltpu.VMEM((8, T, T), F32),
            pltpu.VMEM((SLOTS, ROWS), jnp.int32),
            pltpu.VMEM((ROWS, 128), jnp.int32),
            pltpu.SMEM((ROWS, 128), jnp.int32),
            dma((11,)), dma((4,)),
            dma((32,)), dma((32,)),
            dma((16,)), dma((16,)),
            dma((52,)), dma((52,)),
            dma((32,)), dma((32,)),
            dma((64,)), dma((64,)),
        ],
        compiler_params=pltpu.CompilerParams(
            collective_id=0, has_side_effects=True, vmem_limit_bytes=62 * 1024 * 1024
        ),
        cost_estimate=pl.CostEstimate(flops=6_442_450_944, bytes_accessed=10_000_000, transcendentals=0),
    )(a_cols.T, a_vals.reshape(NSLOT, T, T), p_vals)


def solution(mesh):
    return jax.shard_map(
        per_device,
        mesh=mesh,
        in_specs=(P("row", "col", None, None), P("row", "col"), P(("row", "col"), None, None)),
        out_specs=P("row", "col"),
        check_vma=False,
    )
```

```python
import functools

import jax
import jax.numpy as jnp
from jax import lax
from jax.experimental import pallas as pl
from jax.experimental.pallas import tpu as pltpu
from jax.sharding import PartitionSpec as P

MESH = pl.DeviceIdType.MESH
NX, NY, NZ = 4, 4, 8
T = 256
SLOTS = 4
ROWS = 16
NSLOT = ROWS * SLOTS
HALF, QUART = T // 2, T // 4
UNITS = ((0, 0), (1, 0), (0, 1), (1, 1))
F32 = jnp.float32
BF16 = jnp.bfloat16


def place():
    row, col = lax.axis_index("row"), lax.axis_index("col")
    return row // NX, row % NX, col // 2, col % 2


def chain(cols_ref, links_ref, z, core):
    def order_of(owner, k):
        dist = (owner // 2 - z + NZ) % NZ
        back = jnp.where(dist > NZ // 2, 1, 0)
        near = jnp.minimum(dist, NZ - dist)
        return ((near * 2 + back) * 2 + (owner + core) % 2) * SLOTS + k

    shape = (ROWS, ROWS)
    down = lax.broadcasted_iota(jnp.int32, shape, 0)
    across = lax.broadcasted_iota(jnp.int32, shape, 1)
    turned = [jnp.broadcast_to(cols_ref[k:k + 1, :], shape) for k in range(SLOTS)]
    cols = [jnp.broadcast_to(jnp.sum(jnp.where(down == across, c, 0), axis=1, keepdims=True), shape) for c in turned]
    for k in range(SLOTS + 1):
        asked = cols[k] if k < SLOTS else down
        before = order_of(down, k) if k < SLOTS else jnp.full(shape, 1024, jnp.int32)
        best = jnp.full(shape, -1, jnp.int32)
        for j in range(SLOTS):
            order = order_of(across, j)
            hit = (turned[j] == asked) & (order < before)
            best = jnp.maximum(best, jnp.where(hit, order * NSLOT + across * SLOTS + j, -1))
        best = jnp.max(best, axis=1, keepdims=True)
        links_ref[:, k:k + 1] = jnp.where(best < 0, NSLOT, best % NSLOT)


def kernel(cols_hbm, a_hbm, p_hbm, out_hbm, out_ref, run, a, pt, pc, xr, rcv, first, acc, cols, links, link_ref,
           load_sem, out_sem, zs, zr, hs, hr, ws, wr, xs_sem, xr_sem, ss, sr):
    y, x, z, core = place()
    row, col = y * NX + x, z * 2 + core

    def zdev(step):
        return (row, ((z + step + NZ) % NZ) * 2 + core)

    def sibling():
        return (row, z * 2 + (1 - core))

    def xdev(step):
        return (y * NX + (x + step + NX) % NX, col)

    def ydev(step):
        return (((y + step + NY) % NY) * NX + x, col)

    load_p = [
        pltpu.make_async_copy(p_hbm.at[0, pl.ds((f * 2 + q) * QUART, QUART), pl.ds(n * T, T)], pc.at[n, y, x, f, q], load_sem.at[(n * 2 + f) * 2 + q])
        for n in range(2) for f in range(2) for q in range(2)
    ]
    for c in load_p:
        c.start()
    load_cols = pltpu.make_async_copy(cols_hbm, cols, load_sem.at[9])
    load_cols.start()
    load_a = pltpu.make_async_copy(a_hbm, a, load_sem.at[8])
    load_a.start()

    barrier = pltpu.get_barrier_semaphore()
    partners = [zdev(1), zdev(-1), sibling(), xdev(1), xdev(-1), ydev(1), ydev(-1)]
    for dev in partners:
        pl.semaphore_signal(barrier, inc=1, device_id=dev, device_id_type=MESH)
    for e in range(2):
        run[e, NSLOT] = jnp.zeros((T, T), F32)
        for c in load_p[4 * e:4 * e + 4]:
            c.wait()
        pt[e, col] = pc[e, y, x].reshape(T, T).T
    pl.semaphore_wait(barrier, len(partners))

    result = []
    late = []
    held = ([], [])

    def copy(ref, send_sem, recv_sem, dev, dst=None):
        return pltpu.make_async_remote_copy(
            src_ref=ref, dst_ref=ref if dst is None else dst, send_sem=send_sem, recv_sem=recv_sem,
            device_id=dev, device_id_type=MESH,
        )

    def send(into, *args, **kw):
        c = copy(*args, **kw)
        c.start()
        into.append(c)

    def drain(keep):
        while len(late) > keep:
            late.pop(0).wait_send()

    def zmsg(e, d, hop, q, recv):
        sign = 1 - 2 * d
        back = hop + 1 if recv else hop
        tile = ((z - sign * back + 2 * NZ) % NZ) * 2 + core
        i = ((e * 2 + d) * 4 + hop) * 2 + q
        return pt.at[e, tile, pl.ds(q * HALF, HALF)], zs.at[i], zr.at[i], zdev(sign)

    def zsend(e, hop, k):
        for d in range(2):
            send(held[e], *zmsg(e, d, hop, (d + k) % 2, False))

    def zwait(e, hop, k):
        for d in range(2):
            copy(*zmsg(e, d, hop, (d + k) % 2, True)).wait_recv()

    def hmsg(e, shift, recv):
        tile = ((z + shift + NZ) % NZ) * 2 + ((1 - core) if recv else core)
        i = e * 8 + (shift + NZ) % NZ
        return pt.at[e, tile], hs.at[i], hr.at[i], sibling()

    def hsend(e, *shifts):
        for shift in shifts:
            send(held[e], *hmsg(e, shift, False))

    def hwait(e, *shifts):
        for shift in shifts:
            copy(*hmsg(e, shift, True)).wait_recv()

    def wmsg(n, stage, axis, d, recv):
        sign = 1 - 2 * d
        back = (1 if stage % 2 == 0 else 2) if recv else stage % 2
        along = ((x if axis == 0 else y) - sign * back + 2 * NX) % NX
        across = slice(None) if stage >= 2 else (y if axis == 0 else x)
        half = axis if stage < 2 else 1 - axis
        ref = pc.at[n, across, along, half] if axis == 0 else pc.at[n, along, across, half]
        if stage % 2 == 1:
            ref = ref.at[d] if stage == 1 else ref.at[:, d]
        i = (stage * 2 + axis) * 2 + d
        return ref, ws.at[i], wr.at[i], xdev(sign) if axis == 0 else ydev(sign)

    def wsend(n, stage):
        for axis in range(2):
            for d in range(2):
                send(late, *wmsg(n, stage, axis, d, False))

    def wwait(n, stage):
        for axis in range(2):
            for d in range(2):
                copy(*wmsg(n, stage, axis, d, True)).wait_recv()

    names = {}

    def step_of(axis, amount):
        return (0, amount) if axis == 0 else (amount, 0)

    def wgo(name, axis, d, offset, part, recv):
        sign = 1 - 2 * d
        dy, dx = offset
        if recv:
            sy, sx = step_of(axis, -sign)
            dy, dx = dy + sy, dx + sx
        ref = pc.at[(0, (y + dy + 2 * NY) % NY, (x + dx + 2 * NX) % NX) + part]
        i = 16 + names.setdefault((axis, d) + name, len(names))
        m = (ref, ws.at[i], wr.at[i], xdev(sign) if axis == 0 else ydev(sign))
        if recv:
            copy(*m).wait_recv()
        else:
            send(late, *m)

    both = [(axis, d) for axis in range(2) for d in range(2)]

    def w_own(recv):
        for axis, d in both:
            wgo(("own",), axis, d, (0, 0), (), recv)

    def w_line2(recv):
        for axis, d in both:
            for f in range(2):
                wgo(("line2", f), axis, d, step_of(axis, 2 * d - 1), (f, d), recv)

    def w_diag(o, recv):
        for axis, d in both:
            wgo(("diag", o), axis, d, step_of(1 - axis, o), (1 - axis,), recv)

    def w_diag2(o, recv):
        for axis, d in both:
            ay, ax = step_of(axis, 2 * d - 1)
            by, bx = step_of(1 - axis, o)
            wgo(("diag2", o), axis, d, (ay + by, ax + bx), (1 - axis, d), recv)

    def left(e, dist, lo, hi):
        @pl.loop(lo, hi)
        def _(m):
            tile = ((z + dist * (1 - 2 * (m // 2)) + NZ) % NZ) * 2 + (core + m) % 2
            for k in range(SLOTS):
                s = tile * SLOTS + k
                prev = link_ref[tile, k]
                run[e, s] = run[e, prev] + jnp.dot(pt[e, tile], a[s], preferred_element_type=F32)

    def product(e, n, block):
        last = link_ref[block, SLOTS]
        return jnp.dot(run[e, last].astype(BF16), pc[n, block // NX, block % NX].reshape(T, T), preferred_element_type=F32)

    def block_of(shift, k):
        return ((z + shift + NZ) % NZ) * 2 + k

    def xmsg(u, shift):
        m = (shift + NZ) % NZ
        e, n = UNITS[u]
        i = u * 8 + m
        return pt.at[e, n * 8 + m], xs_sem.at[i], xr_sem.at[i], sibling(), xr.at[i]

    def exchange(u, *shifts):
        e, n = UNITS[u]
        for shift in shifts:
            pt[e, n * 8 + (shift + NZ) % NZ] = product(e, n, block_of(shift, 1 - core)).astype(BF16)
            send(late, *xmsg(u, shift))

    def own(u, shift):
        e, n = UNITS[u]
        value = product(e, n, block_of(shift, core))
        copy(*xmsg(u, shift)).wait_recv()
        return value + xr[u * 8 + (shift + NZ) % NZ].astype(F32)

    def rmsg(u, d, hop, r):
        i = (u * 2 + d) * 4 + hop
        buf = first.at[i] if u == 0 else a.at[i - 8]
        rows = pl.ds(r * HALF, HALF)
        return buf.at[rows], ss.at[i * 2 + r], sr.at[i * 2 + r], zdev(1 - 2 * d), rcv.at[i, rows]

    def pass_on(u, d, hop, r, value):
        m = rmsg(u, d, hop, r)
        m[0][...] = value.astype(BF16)
        send(late, *m)

    def arrived(u, d, hop, r):
        copy(*rmsg(u, d, hop, r)).wait_recv()
        return rcv[(u * 2 + d) * 4 + hop, pl.ds(r * HALF, HALF)].astype(F32)

    def ring(u, step):
        e, n = UNITS[u]
        slot = u * 2
        hop = (step + 1) // 2
        if step == 0:
            total = own(u, 4)
            for d in range(2):
                pass_on(u, d, 0, d, total[d * HALF:(d + 1) * HALF])
            return
        if step == 7:
            out_ref[pl.ds(e * T, T), pl.ds(n * T, T)] = own(u, 0)
        elif step % 2 == 1:
            for d in range(2):
                acc[slot + d] = own(u, (4 - hop) * (1 - 2 * d))
        for d in range(2):
            r = 1 - d if step % 2 == 1 else d
            if step >= 7:
                rows = pl.ds(e * T + r * HALF, HALF), pl.ds(n * T, T)
                out_ref[rows] = out_ref[rows] + arrived(u, d, 3, r)
                continue
            total = acc[slot + d, pl.ds(r * HALF, HALF)]
            if step > 1:
                total = total + arrived(u, d, hop - 1, r)
            pass_on(u, d, hop, r, total)
        if step == 8:
            tile = pl.ds(e * T, T), pl.ds(n * T, T)
            result.append(pltpu.make_async_copy(out_ref.at[tile], out_hbm.at[tile], out_sem.at[u]))
            result[-1].start()

    zsend(0, 0, 0)
    zsend(0, 0, 1)
    hsend(0, 0)
    w_own(False)
    zsend(1, 0, 0)
    zsend(1, 0, 1)
    hsend(1, 0)
    load_cols.wait()
    chain(cols, links, z, core)
    to_scalars = pltpu.make_async_copy(links, link_ref, load_sem.at[10])
    to_scalars.start()
    load_a.wait()
    to_scalars.wait()
    hwait(0, 0)
    left(0, 0, 0, 2)
    zwait(0, 0, 0)
    zsend(0, 1, 0)
    zwait(0, 0, 1)
    zsend(0, 1, 1)
    hsend(0, 1, -1)
    w_own(True)
    w_line2(False)
    w_diag(-1, False)
    w_diag(1, False)
    zwait(1, 0, 0)
    zsend(1, 1, 0)
    zwait(1, 0, 1)
    zsend(1, 1, 1)
    hsend(1, 1, -1)
    hwait(0, 1, -1)
    left(0, 1, 0, 4)
    hwait(1, 0)
    left(1, 0, 0, 2)
    zwait(0, 1, 0)
    zsend(0, 2, 0)
    zwait(0, 1, 1)
    zsend(0, 2, 1)
    hsend(0, 2, -2)
    w_line2(True)
    w_diag(2, False)
    wsend(1, 0)
    hwait(1, 1, -1)
    left(1, 1, 0, 4)
    zwait(1, 1, 0)
    zsend(1, 2, 0)
    zwait(1, 1, 1)
    zsend(1, 2, 1)
    hsend(1, 2, -2)
    w_diag(-1, True)
    w_diag(1, True)
    w_diag2(-1, False)
    w_diag2(1, False)
    hwait(0, 2, -2)
    left(0, 2, 0, 4)
    zwait(0, 2, 0)
    zsend(0, 3, 0)
    zwait(0, 2, 1)
    hsend(0, 3, -3)
    w_diag(2, True)
    w_diag2(2, False)
    wwait(1, 0)
    wsend(1, 1)
    hwait(1, 2, -2)
    left(1, 2, 0, 4)
    hwait(0, 3, -3)
    left(0, 3, 0, 4)
    zwait(1, 2, 0)
    zsend(1, 3, 0)
    zwait(1, 2, 1)
    hsend(1, 3, -3)
    zwait(0, 3, 0)
    hsend(0, 4)
    left(0, 4, 0, 1)
    hwait(0, 4)
    left(0, 4, 1, 2)
    for c in held[0]:
        c.wait_send()
    w_diag2(-1, True)
    w_diag2(1, True)
    w_diag2(2, True)
    exchange(0, 4, 3, -3)
    hwait(1, 3, -3)
    left(1, 3, 0, 2)
    ring(0, 0)
    ring(0, 1)
    wwait(1, 1)
    wsend(1, 2)
    zwait(1, 3, 0)
    hsend(1, 4)
    left(1, 3, 2, 4)
    left(1, 4, 0, 1)
    hwait(1, 4)
    left(1, 4, 1, 2)
    for c in held[1]:
        c.wait_send()
    exchange(1, 4, 3, -3)
    ring(1, 0)
    ring(1, 1)
    exchange(0, 2, -2)
    ring(0, 2)
    ring(0, 3)
    exchange(1, 2, -2)
    exchange(0, 1, -1)
    ring(1, 2)
    ring(1, 3)
    wwait(1, 2)
    wsend(1, 3)
    ring(0, 4)
    exchange(1, 1, -1)
    ring(0, 5)
    ring(0, 6)
    wwait(1, 3)
    exchange(2, 4, 3, -3)
    ring(1, 4)
    ring(2, 0)
    exchange(3, 4, 3, -3)
    ring(2, 1)
    exchange(2, 2, -2)
    ring(3, 0)
    ring(3, 1)
    exchange(3, 2, -2)
    ring(1, 5)
    exchange(0, 0)
    ring(2, 2)
    ring(3, 2)
    exchange(2, 1, -1)
    ring(1, 6)
    ring(2, 3)
    exchange(3, 1, -1)
    ring(3, 3)
    exchange(1, 0)
    ring(0, 7)
    ring(0, 8)
    exchange(2, 0)
    ring(2, 4)
    ring(3, 4)
    exchange(3, 0)
    ring(2, 5)
    ring(3, 5)
    ring(1, 7)
    ring(1, 8)
    ring(2, 6)
    ring(3, 6)
    ring(2, 7)
    ring(3, 7)
    ring(2, 8)
    ring(3, 8)
    drain(0)
    for c in result:
        c.wait()


def hand_over(src, dst, via, into, out):
    parts = [pl.ds(i * QUART, QUART) for i in range(8)]
    come = [pltpu.make_async_copy(src.at[r], via.at[r], into.at[i]) for i, r in enumerate(parts)]
    go = [pltpu.make_async_copy(via.at[r], dst.at[r], out.at[i]) for i, r in enumerate(parts)]
    for c in come:
        c.start()
    for c, g in zip(come, go):
        c.wait()
        g.start()
    for g in go:
        g.wait()


def per_device(a_vals, a_cols, p_vals):
    dma = pltpu.SemaphoreType.DMA
    coarse = pl.pallas_call(
        kernel,
        out_shape=jax.ShapeDtypeStruct((2 * T, 2 * T), F32),
        in_specs=[
            pl.BlockSpec(memory_space=pl.ANY),
            pl.BlockSpec(memory_space=pl.ANY),
            pl.BlockSpec(memory_space=pl.ANY),
        ],
        out_specs=pl.BlockSpec(memory_space=pl.ANY),
        scratch_shapes=[
            pltpu.VMEM((2 * T, 2 * T), F32),
            pltpu.VMEM((2, NSLOT + 1, T, T), F32),
            pltpu.VMEM((NSLOT, T, T), BF16),
            pltpu.VMEM((2, ROWS, T, T), BF16),
            pltpu.VMEM((2, NY, NX, 2, 2, QUART, T), BF16),
            pltpu.VMEM((32, T, T), BF16),
            pltpu.VMEM((32, T, T), BF16),
            pltpu.VMEM((8, T, T), BF16),
            pltpu.VMEM((8, T, T), F32),
            pltpu.VMEM((SLOTS, ROWS), jnp.int32),
            pltpu.VMEM((ROWS, 128), jnp.int32),
            pltpu.SMEM((ROWS, 128), jnp.int32),
            dma((11,)), dma((4,)),
            dma((32,)), dma((32,)),
            dma((16,)), dma((16,)),
            dma((52,)), dma((52,)),
            dma((32,)), dma((32,)),
            dma((64,)), dma((64,)),
        ],
        compiler_params=pltpu.CompilerParams(
            collective_id=0, has_side_effects=True, vmem_limit_bytes=62 * 1024 * 1024
        ),
        cost_estimate=pl.CostEstimate(flops=6_442_450_944, bytes_accessed=10_000_000, transcendentals=0),
    )(a_cols.T, a_vals.reshape(NSLOT, T, T), p_vals)
    return pl.pallas_call(
        hand_over,
        out_shape=jax.ShapeDtypeStruct((2 * T, 2 * T), F32),
        in_specs=[pl.BlockSpec(memory_space=pl.ANY)],
        out_specs=pl.BlockSpec(memory_space=pl.ANY),
        scratch_shapes=[pltpu.VMEM((2 * T, 2 * T), F32), dma((8,)), dma((8,))],
    )(coarse)


def solution(mesh):
    return jax.shard_map(
        per_device,
        mesh=mesh,
        in_specs=(P("row", "col", None, None), P("row", "col"), P(("row", "col"), None, None)),
        out_specs=P("row", "col"),
        check_vma=False,
    )
```
